32 devices in a mesh: section: 16 (over z, y, core), band: 2 (over x).
Axes of the slice: x: 2, y: 2, z: 4, core: 2. Of those that a mesh axis runs over, the one named last changes fastest.
Arguments:
- section_inputs: bfloat16 [16, 2, 16, 64, 256], P('section', None, 'band'), may hold values from -6 to 6
- skip_inputs: bfloat16 [16, 2, 16, 64, 256], P('section', None, 'band'), may hold values from -6 to 6
- fresh_batches: bfloat16 [2, 2, 16, 64, 256], P(None, None, 'band'), may hold values from -6 to 6
- first_weights: bfloat16 [16, 3, 3, 256, 256], P('section'), may hold values from -0.1875 to 0.1875
- skip_weights: bfloat16 [16, 3, 3, 256, 256], P('section'), may hold values from -0.1875 to 0.1875
- second_weights: bfloat16 [16, 3, 3, 256, 256], P('section'), may hold values from -0.1875 to 0.1875
Outputs:
- produced: bfloat16 [16, 2, 16, 64, 256], P('section', None, 'band')
- mirrored: bfloat16 [16, 2, 16, 64, 256], P('section', None, 'band')
The draws below stay inside these ranges and needn't reach their ends.
All inputs are finite; a program needn't handle non-finite values.
Results may differ from the reference program's by a relative error of at most 0.012.
Values may be sent and summed in bfloat16 or wider, within the bound.
A program may use at most 64 MiB of HBM per device.

```python
import jax
import jax.numpy as jnp
from jax import lax

C = 256
WIDTH = 64
MB = 2
TICKS = 3
SECTIONS = 16
HEIGHT = 16


def level_of(key, shape, pieces, low, top_value):
    factor_of = 1.0
    for dim, parts in pieces:
        steps = jax.random.uniform(jax.random.fold_in(jax.random.fold_in(key, 6), dim), (parts,), jnp.float32, low / len(pieces), top_value / len(pieces))
        factor_of = factor_of * jnp.repeat(jnp.exp(steps), shape[dim] // parts).reshape((-1,) + (1,) * (len(shape) - 1 - dim))
    return factor_of


def centred(own_key, dims, spread, bound, shards=(), dtype=jnp.bfloat16):
    entries = jax.random.normal(own_key, dims, jnp.float32) * spread
    if len(shards) > 0:
        entries = level_of(own_key, dims, shards, -0.22, 0.18) * entries
    return jnp.clip(entries, min=-bound, max=bound).astype(dtype)


def setup_inputs(seed: int = 0) -> dict:
    splits = jax.random.split(jax.random.key(seed), 7)
    return {
        "section_inputs": centred(splits[0], (SECTIONS, MB, HEIGHT, WIDTH, C), 1.0, 6.0, ((0, 16), (2, 2))),
        "skip_inputs": centred(splits[1], (SECTIONS, MB, HEIGHT, WIDTH, C), 1.0, 6.0, ((0, 16), (2, 2))),
        "fresh_batches": centred(splits[2], (TICKS - 1, MB, HEIGHT, WIDTH, C), 1.0, 6.0, ((2, 2),)),
        "first_weights": centred(splits[3], (SECTIONS, 3, 3, C, C), ((2.0 / (9 * C)) ** 0.5), 0.1875, ((0, 16),)),
        "skip_weights": centred(splits[4], (SECTIONS, 3, 3, C, C), ((2.0 / (9 * C)) ** 0.5), 0.1875, ((0, 16),)),
        "second_weights": centred(splits[5], (SECTIONS, 3, 3, C, C), ((2.0 / (9 * C)) ** 0.5), 0.1875, ((0, 16),)),
    }


def conv_rows(padded, weight, out_rows):
    width = padded.shape[2]
    wide = jnp.pad(padded, ((0, 0), (0, 0), (1, 1), (0, 0)))
    total = jnp.zeros((padded.shape[0], out_rows, width, weight.shape[3]), jnp.float32)
    for row_shift in range(3):
        for col_shift in range(3):
            window = wide[:, row_shift:row_shift + out_rows, col_shift:col_shift + width, :]
            flat = window.reshape(-1, window.shape[3])
            product = jnp.dot(flat, weight[row_shift, col_shift], preferred_element_type=jnp.float32)
            total = total + product.reshape(total.shape)
    return total


def section_block(current, mirrored, first_weight, skip_weight, second_weight, decoder):
    rows = current.shape[1]
    pad_rows = ((0, 0), (1, 1), (0, 0), (0, 0))
    first_sum = conv_rows(jnp.pad(current, pad_rows), first_weight, rows)
    first_sum = first_sum + decoder * conv_rows(jnp.pad(mirrored, pad_rows), skip_weight, rows)
    hidden = jax.nn.relu(first_sum).astype(jnp.bfloat16)
    second_sum = conv_rows(jnp.pad(hidden, pad_rows), second_weight, rows)
    return jax.nn.relu(second_sum).astype(jnp.bfloat16)


def reference(section_inputs, skip_inputs, fresh_batches, first_weights, skip_weights, second_weights):
    sections = first_weights.shape[0]
    decoder_flags = (jnp.arange(sections) >= sections // 2).astype(jnp.float32)
    current = section_inputs
    mirrored = skip_inputs
    produced = section_inputs
    for tick_index in range(TICKS):
        produced = lax.map(lambda items: section_block(*items), (current, mirrored, first_weights, skip_weights, second_weights, decoder_flags))
        mirrored = produced[::-1]
        if tick_index + 1 < TICKS:
            current = jnp.concatenate([fresh_batches[tick_index][None], produced[:-1]], axis=0)
    return produced, mirrored
```

```python
import functools

import jax
import jax.numpy as jnp
from jax import lax
from jax.experimental import pallas as pl
from jax.experimental.pallas import tpu as pltpu
from jax.sharding import PartitionSpec as P

MESH = pl.DeviceIdType.MESH
HALO = 2


def conv_rows(x, w_ref, out_rows, width):
    size = out_rows * width
    rows_of_k = jnp.concatenate([x[a * width : a * width + size] for a in range(3)], axis=1)
    total = None
    for b in (1, 0, 2):
        weight = jnp.concatenate([w_ref[a * 3 + b] for a in range(3)], axis=0)
        part = jnp.dot(rows_of_k, weight, preferred_element_type=jnp.float32)
        if b == 1:
            total = part
            continue
        column = lax.broadcasted_iota(jnp.int32, part.shape, 0) % width
        if b == 0:
            total = total + jnp.where(column == 0, 0.0, pltpu.roll(part, 1, 0))
        else:
            total = total + jnp.where(column == width - 1, 0.0, pltpu.roll(part, size - 1, 0))
    return total


def kernel(
    sections, bands, width,
    cur_in, skip_in, fresh_in, w1_in, ws_in, w2_in,
    produced_out, mirrored_out,
    w1, ws, w2, cur, mir, made, acc, hid,
    load_w, load_cur, load_mir, store_out,
    send_next, recv_next, send_mirror, recv_mirror,
    send_up, recv_below, send_down, recv_above,
):
    s = lax.axis_index("section")
    b = lax.axis_index("band")
    is_decoder = s >= sections // 2
    ticks, images = made.shape[0], made.shape[1]
    own = made.shape[2]
    edge = HALO * width
    rows = own // width
    mirror = sections - 1 - s
    has_up, has_down = b > 0, b < bands - 1
    has_prev, has_next = s > 0, s < sections - 1
    middle = pl.ds(edge, own)
    above, below = pl.ds(0, edge), pl.ds(edge + own, edge)

    load_weights = [
        pltpu.make_async_copy(source, target, load_w.at[k])
        for k, (source, target) in enumerate(((w1_in, w1), (w2_in, w2), (ws_in, ws)))
    ]
    load_curs = [
        pltpu.make_async_copy(cur_in.at[i], cur.at[0, i, middle], load_cur.at[0, i])
        for i in range(images)
    ]
    load_mirs = [
        pltpu.make_async_copy(skip_in.at[i], mir.at[0, i, middle], load_mir.at[i])
        for i in range(images)
    ]
    load_fresh = {
        (t, i): pltpu.make_async_copy(
            fresh_in.at[t - 1, i], cur.at[t, i, middle], load_cur.at[t, i]
        )
        for t in range(1, ticks)
        for i in range(images)
    }
    load_curs[0].start()
    load_weights[0].start()
    load_weights[1].start()
    for copy in load_curs[1:]:
        copy.start()

    @pl.when(is_decoder)
    def _():
        load_weights[2].start()
        for copy in load_mirs:
            copy.start()

    @pl.when(s == 0)
    def _():
        for copy in load_fresh.values():
            copy.start()

    barrier = pltpu.get_barrier_semaphore()

    def greet(condition, device):
        @pl.when(condition)
        def _():
            pl.semaphore_signal(barrier, inc=1, device_id=device, device_id_type=MESH)

    greet(has_up, (s, b - 1))
    greet(has_down, (s, b + 1))
    greet(has_prev, (s - 1, b))
    greet(has_next, (s + 1, b))
    pl.semaphore_signal(barrier, inc=1, device_id=(mirror, b), device_id_type=MESH)

    blank = jnp.zeros((edge, cur.shape[3]), cur.dtype)

    @pl.when(jnp.logical_not(has_up))
    def _():
        for t in range(ticks):
            for i in range(images):
                cur[t, i, 0:edge] = blank
                mir[t, i, 0:edge] = blank

    @pl.when(jnp.logical_not(has_down))
    def _():
        for t in range(ticks):
            for i in range(images):
                cur[t, i, edge + own : edge + own + edge] = blank
                mir[t, i, edge + own : edge + own + edge] = blank

    greeted = (
        1
        + has_up.astype(jnp.int32)
        + has_down.astype(jnp.int32)
        + has_prev.astype(jnp.int32)
        + has_next.astype(jnp.int32)
    )
    pl.semaphore_wait(barrier, greeted)

    def to_up(kind, array, t, i, source):
        return pltpu.make_async_remote_copy(
            src_ref=source,
            dst_ref=array.at[t, i, below],
            send_sem=send_up.at[kind, t, i],
            recv_sem=recv_below.at[kind, t, i],
            device_id=(s, b - 1),
            device_id_type=MESH,
        )

    def to_down(kind, array, t, i, source):
        return pltpu.make_async_remote_copy(
            src_ref=source,
            dst_ref=array.at[t, i, above],
            send_sem=send_down.at[kind, t, i],
            recv_sem=recv_above.at[kind, t, i],
            device_id=(s, b + 1),
            device_id_type=MESH,
        )

    def give_edges(kind, array, t, i, source, first):
        @pl.when(has_up)
        def _():
            to_up(kind, array, t, i, source.at[pl.ds(first, edge)]).start()

        @pl.when(has_down)
        def _():
            to_down(kind, array, t, i, source.at[pl.ds(first + own - edge, edge)]).start()

    def await_edges(kind, array, t, i):
        @pl.when(has_up)
        def _():
            to_down(kind, array, t, i, array.at[t, i, above]).wait_recv()

        @pl.when(has_down)
        def _():
            to_up(kind, array, t, i, array.at[t, i, below]).wait_recv()

    def finish_edges(kind, array, t, i):
        @pl.when(has_up)
        def _():
            to_up(kind, array, t, i, array.at[t, i, above]).wait_send()

        @pl.when(has_down)
        def _():
            to_down(kind, array, t, i, array.at[t, i, below]).wait_send()

    def to_next(t, i):
        return pltpu.make_async_remote_copy(
            src_ref=made.at[t, i],
            dst_ref=cur.at[t + 1, i, middle],
            send_sem=send_next.at[t, i],
            recv_sem=recv_next.at[t, i],
            device_id=(s + 1, b),
            device_id_type=MESH,
        )

    def to_mirror(t, i):
        last = t + 1 == ticks
        return pltpu.make_async_remote_copy(
            src_ref=made.at[t, i],
            dst_ref=mirrored_out.at[i] if last else mir.at[t + 1, i, middle],
            send_sem=send_mirror.at[t, i],
            recv_sem=recv_mirror.at[t, i],
            device_id=(mirror, b),
            device_id_type=MESH,
        )

    for i in range(images):
        give_edges(0, cur, 0, i, cur_in.at[i], 0)

        @pl.when(is_decoder)
        def _():
            give_edges(1, mir, 0, i, skip_in.at[i], 0)

    @pl.when(s == 0)
    def _():
        for t in range(1, ticks):
            for i in range(images):
                give_edges(0, cur, t, i, fresh_in.at[t - 1, i], 0)

    for t in range(ticks):
        for i in range(images):
            if t == 0:
                load_curs[i].wait()
            else:

                @pl.when(s == 0)
                def _():
                    load_fresh[t, i].wait()

                @pl.when(has_prev)
                def _():
                    to_next(t - 1, i).wait_recv()
                    give_edges(0, cur, t, i, cur.at[t, i], edge)

            if t == 0 and i == 0:
                load_weights[0].wait()
            await_edges(0, cur, t, i)
            acc[...] = conv_rows(cur[t, i], w1, rows + HALO, width)

            @pl.when(is_decoder)
            def _():
                if t == 0:
                    if i == 0:
                        load_weights[2].wait()
                    load_mirs[i].wait()
                else:
                    to_mirror(t - 1, i).wait_recv()
                    give_edges(1, mir, t, i, mir.at[t, i], edge)
                await_edges(1, mir, t, i)
                acc[...] += conv_rows(mir[t, i], ws, rows + HALO, width)

            hid[...] = jnp.maximum(acc[...], 0.0).astype(hid.dtype)
            nothing = jnp.zeros((width, hid.shape[1]), hid.dtype)

            @pl.when(jnp.logical_not(has_up))
            def _():
                hid[0:width] = nothing

            @pl.when(jnp.logical_not(has_down))
            def _():
                hid[width + own : width + own + width] = nothing

            if t == 0 and i == 0:
                load_weights[1].wait()
            made[t, i] = jnp.maximum(conv_rows(hid[...], w2, rows, width), 0.0).astype(made.dtype)
            if t + 1 < ticks:

                @pl.when(has_next)
                def _():
                    to_next(t, i).start()

                @pl.when(jnp.logical_not(is_decoder))
                def _():
                    to_mirror(t, i).start()
            else:
                to_mirror(t, i).start()
                pltpu.make_async_copy(made.at[t, i], produced_out.at[i], store_out.at[i]).start()

    for i in range(images):
        pltpu.make_async_copy(made.at[ticks - 1, i], produced_out.at[i], store_out.at[i]).wait()
        for t in range(ticks):
            finish_edges(0, cur, t, i)

            @pl.when(is_decoder)
            def _():
                finish_edges(1, mir, t, i)

            if t + 1 < ticks:

                @pl.when(has_next)
                def _():
                    to_next(t, i).wait_send()

                @pl.when(jnp.logical_not(is_decoder))
                def _():
                    to_mirror(t, i).wait_send()
            else:
                to_mirror(t, i).wait_send()
                to_mirror(t, i).wait_recv()


def body(section_inputs, skip_inputs, fresh_batches, first_weights, skip_weights, second_weights):
    sections = lax.axis_size("section")
    bands = lax.axis_size("band")
    _, images, rows, width, channels = section_inputs.shape
    ticks = fresh_batches.shape[0] + 1
    own = rows * width
    padded = (rows + 2 * HALO) * width
    dtype = section_inputs.dtype
    out = jax.ShapeDtypeStruct((images, own, channels), dtype)
    taps = (9, channels, channels)
    dma = pltpu.SemaphoreType.DMA
    flops = 2 * ticks * images * own * 9 * channels * channels * 3
    produced, mirrored = pl.pallas_call(
        functools.partial(kernel, sections, bands, width),
        out_shape=(out, out),
        in_specs=[pl.BlockSpec(memory_space=pl.ANY)] * 6,
        out_specs=(pl.BlockSpec(memory_space=pl.ANY),) * 2,
        scratch_shapes=[
            pltpu.VMEM(taps, dtype),
            pltpu.VMEM(taps, dtype),
            pltpu.VMEM(taps, dtype),
            pltpu.VMEM((ticks, images, padded, channels), dtype),
            pltpu.VMEM((ticks, images, padded, channels), dtype),
            pltpu.VMEM((ticks, images, own, channels), dtype),
            pltpu.VMEM(((rows + HALO) * width, channels), jnp.float32),
            pltpu.VMEM(((rows + HALO) * width, channels), dtype),
            dma((3,)),
            dma((ticks, images)),
            dma((images,)),
            dma((images,)),
            dma((ticks, images)),
            dma((ticks, images)),
            dma((ticks, images)),
            dma((ticks, images)),
            dma((2, ticks, images)),
            dma((2, ticks, images)),
            dma((2, ticks, images)),
            dma((2, ticks, images)),
        ],
        compiler_params=pltpu.CompilerParams(
            collective_id=0, has_side_effects=True, vmem_limit_bytes=48 * 1024 * 1024
        ),
        cost_estimate=pl.CostEstimate(flops=flops, bytes_accessed=8 * 2**20, transcendentals=0),
    )(
        section_inputs.reshape(images, own, channels),
        skip_inputs.reshape(images, own, channels),
        fresh_batches.reshape(ticks - 1, images, own, channels),
        first_weights.reshape(taps),
        skip_weights.reshape(taps),
        second_weights.reshape(taps),
    )
    shape = section_inputs.shape
    return produced.reshape(shape), mirrored.reshape(shape)


def solution(mesh):
    in_specs = (
        P("section", None, "band", None, None),
        P("section", None, "band", None, None),
        P(None, None, "band", None, None),
        P("section", None, None, None, None),
        P("section", None, None, None, None),
        P("section", None, None, None, None),
    )
    out_specs = (P("section", None, "band", None, None), P("section", None, "band", None, None))
    return jax.shard_map(body, mesh=mesh, in_specs=in_specs, out_specs=out_specs, check_vma=False)
```

```python
import functools

import jax
import jax.numpy as jnp
from jax import lax
from jax.experimental import pallas as pl
from jax.experimental.pallas import tpu as pltpu
from jax.sharding import PartitionSpec as P

MESH = pl.DeviceIdType.MESH
HALO = 2


def conv_rows(x, w_ref, out_rows, width):
    size = out_rows * width
    rows_of_k = jnp.concatenate([x[a * width : a * width + size] for a in range(3)], axis=1)
    total = None
    for b in (1, 0, 2):
        weight = jnp.concatenate([w_ref[a * 3 + b] for a in range(3)], axis=0)
        part = jnp.dot(rows_of_k, weight, preferred_element_type=jnp.float32)
        if b == 1:
            total = part
            continue
        column = lax.broadcasted_iota(jnp.int32, part.shape, 0) % width
        if b == 0:
            total = total + jnp.where(column == 0, 0.0, pltpu.roll(part, 1, 0))
        else:
            total = total + jnp.where(column == width - 1, 0.0, pltpu.roll(part, size - 1, 0))
    return total


def kernel(
    sections, bands, width,
    cur_in, skip_in, fresh_in, w1_in, ws_in, w2_in,
    produced_out, mirrored_out,
    w1, ws, w2, cur, mir, made, acc, hid,
    load_w, load_cur, load_mir, store_out,
    send_next, recv_next, send_mirror, recv_mirror,
    send_up, recv_below, send_down, recv_above,
):
    s = lax.axis_index("section")
    b = lax.axis_index("band")
    is_decoder = s >= sections // 2
    joined_decoder = s == sections // 2
    sends_mirror = s < sections // 2 - 1
    takes_mirror = s > sections // 2
    ticks, images = made.shape[0], made.shape[1]
    own = made.shape[2]
    edge = HALO * width
    rows = own // width
    mirror = sections - 1 - s
    has_up, has_down = b > 0, b < bands - 1
    has_prev, has_next = s > 0, s < sections - 1
    middle = pl.ds(edge, own)
    above, below = pl.ds(0, edge), pl.ds(edge + own, edge)

    load_weights = [
        pltpu.make_async_copy(source, target, load_w.at[k])
        for k, (source, target) in enumerate(((w1_in, w1), (w2_in, w2), (ws_in, ws)))
    ]
    load_curs = [
        pltpu.make_async_copy(cur_in.at[i], cur.at[0, i, middle], load_cur.at[0, i])
        for i in range(images)
    ]
    load_mirs = [
        pltpu.make_async_copy(skip_in.at[i], mir.at[0, i, middle], load_mir.at[i])
        for i in range(images)
    ]
    load_fresh = {
        (t, i): pltpu.make_async_copy(
            fresh_in.at[t - 1, i], cur.at[t, i, middle], load_cur.at[t, i]
        )
        for t in range(1, ticks)
        for i in range(images)
    }
    load_curs[0].start()
    load_weights[0].start()
    load_weights[1].start()
    for copy in load_curs[1:]:
        copy.start()

    @pl.when(is_decoder)
    def _():
        load_weights[2].start()
        for copy in load_mirs:
            copy.start()

    @pl.when(s == 0)
    def _():
        for copy in load_fresh.values():
            copy.start()

    barrier = pltpu.get_barrier_semaphore()

    def greet(condition, device):
        @pl.when(condition)
        def _():
            pl.semaphore_signal(barrier, inc=1, device_id=device, device_id_type=MESH)

    greet(has_up, (s, b - 1))
    greet(has_down, (s, b + 1))
    greet(has_prev, (s - 1, b))
    greet(has_next, (s + 1, b))
    pl.semaphore_signal(barrier, inc=1, device_id=(mirror, b), device_id_type=MESH)

    blank = jnp.zeros((edge, cur.shape[3]), cur.dtype)

    @pl.when(jnp.logical_not(has_up))
    def _():
        for t in range(ticks):
            for i in range(images):
                cur[t, i, 0:edge] = blank
                mir[t, i, 0:edge] = blank

    @pl.when(jnp.logical_not(has_down))
    def _():
        for t in range(ticks):
            for i in range(images):
                cur[t, i, edge + own : edge + own + edge] = blank
                mir[t, i, edge + own : edge + own + edge] = blank

    greeted = (
        1
        + has_up.astype(jnp.int32)
        + has_down.astype(jnp.int32)
        + has_prev.astype(jnp.int32)
        + has_next.astype(jnp.int32)
    )
    pl.semaphore_wait(barrier, greeted)

    def to_up(kind, array, t, i, source):
        return pltpu.make_async_remote_copy(
            src_ref=source,
            dst_ref=array.at[t, i, below],
            send_sem=send_up.at[kind, t, i],
            recv_sem=recv_below.at[kind, t, i],
            device_id=(s, b - 1),
            device_id_type=MESH,
        )

    def to_down(kind, array, t, i, source):
        return pltpu.make_async_remote_copy(
            src_ref=source,
            dst_ref=array.at[t, i, above],
            send_sem=send_down.at[kind, t, i],
            recv_sem=recv_above.at[kind, t, i],
            device_id=(s, b + 1),
            device_id_type=MESH,
        )

    def give_edges(kind, array, t, i, source, first):
        @pl.when(has_up)
        def _():
            to_up(kind, array, t, i, source.at[pl.ds(first, edge)]).start()

        @pl.when(has_down)
        def _():
            to_down(kind, array, t, i, source.at[pl.ds(first + own - edge, edge)]).start()

    def await_edges(kind, array, t, i):
        @pl.when(has_up)
        def _():
            to_down(kind, array, t, i, array.at[t, i, above]).wait_recv()

        @pl.when(has_down)
        def _():
            to_up(kind, array, t, i, array.at[t, i, below]).wait_recv()

    def finish_edges(kind, array, t, i):
        @pl.when(has_up)
        def _():
            to_up(kind, array, t, i, array.at[t, i, above]).wait_send()

        @pl.when(has_down)
        def _():
            to_down(kind, array, t, i, array.at[t, i, below]).wait_send()

    def to_next(t, i):
        return pltpu.make_async_remote_copy(
            src_ref=made.at[t, i],
            dst_ref=cur.at[t + 1, i, middle],
            send_sem=send_next.at[t, i],
            recv_sem=recv_next.at[t, i],
            device_id=(s + 1, b),
            device_id_type=MESH,
        )

    def to_mirror(t, i):
        last = t + 1 == ticks
        return pltpu.make_async_remote_copy(
            src_ref=made.at[t, i],
            dst_ref=mirrored_out.at[i] if last else mir.at[t + 1, i, middle],
            send_sem=send_mirror.at[t, i],
            recv_sem=recv_mirror.at[t, i],
            device_id=(mirror, b),
            device_id_type=MESH,
        )

    for i in range(images):
        give_edges(0, cur, 0, i, cur_in.at[i], 0)

        @pl.when(is_decoder)
        def _():
            give_edges(1, mir, 0, i, skip_in.at[i], 0)

    @pl.when(s == 0)
    def _():
        for t in range(1, ticks):
            for i in range(images):
                give_edges(0, cur, t, i, fresh_in.at[t - 1, i], 0)

    inner = [(t, i) for i in range(images) for t in range(ticks - 1)]
    outer = [(ticks - 1, i) for i in range(images)]
    pending = list(inner)
    computed = set()
    in_flight = []

    def advance_mirrors():
        while pending and pending[0] in computed:
            step = pending.pop(0)

            @pl.when(sends_mirror)
            def _():
                if in_flight:
                    to_mirror(*in_flight[-1]).wait_send()
                to_mirror(*step).start()

            in_flight.append(step)

    steps = [(0, i) for i in range(images)]
    steps += [(t, i) for i in range(images) for t in range(1, ticks)]
    for t, i in steps:
        if t == 0:
            load_curs[i].wait()
        else:

            @pl.when(s == 0)
            def _():
                load_fresh[t, i].wait()

            @pl.when(has_prev)
            def _():
                to_next(t - 1, i).wait_recv()
                give_edges(0, cur, t, i, cur.at[t, i], edge)

        if t == 0 and i == 0:
            load_weights[0].wait()
        await_edges(0, cur, t, i)
        acc[...] = conv_rows(cur[t, i], w1, rows + HALO, width)

        @pl.when(is_decoder)
        def _():
            if t == 0:
                if i == 0:
                    load_weights[2].wait()
                load_mirs[i].wait()
                await_edges(1, mir, t, i)
            else:

                @pl.when(takes_mirror)
                def _():
                    to_mirror(t - 1, i).wait_recv()
                    give_edges(1, mir, t, i, mir.at[t, i], edge)
                    await_edges(1, mir, t, i)

                @pl.when(joined_decoder)
                def _():
                    mir[t, i] = cur[t, i]

            acc[...] += conv_rows(mir[t, i], ws, rows + HALO, width)

        hid[...] = jnp.maximum(acc[...], 0.0).astype(hid.dtype)
        nothing = jnp.zeros((width, hid.shape[1]), hid.dtype)

        @pl.when(jnp.logical_not(has_up))
        def _():
            hid[0:width] = nothing

        @pl.when(jnp.logical_not(has_down))
        def _():
            hid[width + own : width + own + width] = nothing

        if t == 0 and i == 0:
            load_weights[1].wait()
        made[t, i] = jnp.maximum(conv_rows(hid[...], w2, rows, width), 0.0).astype(made.dtype)
        if t + 1 < ticks:

            @pl.when(has_next)
            def _():
                to_next(t, i).start()

            computed.add((t, i))
            advance_mirrors()
        else:

            @pl.when(is_decoder)
            def _():
                to_mirror(t, i).start()

            pltpu.make_async_copy(made.at[t, i], produced_out.at[i], store_out.at[i]).start()

    @pl.when(jnp.logical_not(is_decoder))
    def _():
        for k, step in enumerate(outer):
            if k == 0:

                @pl.when(sends_mirror)
                def _():
                    to_mirror(*in_flight[-1]).wait_send()

                to_mirror(*step).wait_recv()
            else:
                to_mirror(*outer[k - 1]).wait_send()
            to_mirror(*step).start()

        to_mirror(*outer[-1]).wait_send()
        for step in outer[1:]:
            to_mirror(*step).wait_recv()

    @pl.when(is_decoder)
    def _():
        for step in outer:
            to_mirror(*step).wait_send()
            to_mirror(*step).wait_recv()

    for i in range(images):
        pltpu.make_async_copy(made.at[ticks - 1, i], produced_out.at[i], store_out.at[i]).wait()
        for t in range(ticks):
            finish_edges(0, cur, t, i)

            @pl.when(is_decoder if t == 0 else takes_mirror)
            def _():
                finish_edges(1, mir, t, i)

            if t + 1 < ticks:

                @pl.when(has_next)
                def _():
                    to_next(t, i).wait_send()


def body(section_inputs, skip_inputs, fresh_batches, first_weights, skip_weights, second_weights):
    sections = lax.axis_size("section")
    bands = lax.axis_size("band")
    _, images, rows, width, channels = section_inputs.shape
    ticks = fresh_batches.shape[0] + 1
    own = rows * width
    padded = (rows + 2 * HALO) * width
    dtype = section_inputs.dtype
    out = jax.ShapeDtypeStruct((images, own, channels), dtype)
    taps = (9, channels, channels)
    dma = pltpu.SemaphoreType.DMA
    flops = 2 * ticks * images * own * 9 * channels * channels * 3
    produced, mirrored = pl.pallas_call(
        functools.partial(kernel, sections, bands, width),
        out_shape=(out, out),
        in_specs=[pl.BlockSpec(memory_space=pltpu.HBM)] * 6,
        out_specs=(pl.BlockSpec(memory_space=pltpu.HBM),) * 2,
        scratch_shapes=[
            pltpu.VMEM(taps, dtype),
            pltpu.VMEM(taps, dtype),
            pltpu.VMEM(taps, dtype),
            pltpu.VMEM((ticks, images, padded, channels), dtype),
            pltpu.VMEM((ticks, images, padded, channels), dtype),
            pltpu.VMEM((ticks, images, own, channels), dtype),
            pltpu.VMEM(((rows + HALO) * width, channels), jnp.float32),
            pltpu.VMEM(((rows + HALO) * width, channels), dtype),
            dma((3,)),
            dma((ticks, images)),
            dma((images,)),
            dma((images,)),
            dma((ticks, images)),
            dma((ticks, images)),
            dma((ticks, images)),
            dma((ticks, images)),
            dma((2, ticks, images)),
            dma((2, ticks, images)),
            dma((2, ticks, images)),
            dma((2, ticks, images)),
        ],
        compiler_params=pltpu.CompilerParams(
            collective_id=0, has_side_effects=True, vmem_limit_bytes=48 * 1024 * 1024
        ),
        cost_estimate=pl.CostEstimate(flops=flops, bytes_accessed=8 * 2**20, transcendentals=0),
    )(
        section_inputs.reshape(images, own, channels),
        skip_inputs.reshape(images, own, channels),
        fresh_batches.reshape(ticks - 1, images, own, channels),
        first_weights.reshape(taps),
        skip_weights.reshape(taps),
        second_weights.reshape(taps),
    )
    shape = section_inputs.shape
    return produced.reshape(shape), mirrored.reshape(shape)


def solution(mesh):
    in_specs = (
        P("section", None, "band", None, None),
        P("section", None, "band", None, None),
        P(None, None, "band", None, None),
        P("section", None, None, None, None),
        P("section", None, None, None, None),
        P("section", None, None, None, None),
    )
    out_specs = (P("section", None, "band", None, None), P("section", None, "band", None, None))
    return jax.shard_map(body, mesh=mesh, in_specs=in_specs, out_specs=out_specs, check_vma=False)
```

```python
import functools

import jax
import jax.numpy as jnp
from jax import lax
from jax.experimental import pallas as pl
from jax.experimental.pallas import tpu as pltpu
from jax.sharding import PartitionSpec as P

MESH = pl.DeviceIdType.MESH
HALO = 2


def conv_rows(x, w_ref, out_rows, width):
    size = out_rows * width
    rows_of_k = jnp.concatenate([x[a * width : a * width + size] for a in range(3)], axis=1)
    total = None
    for b in (1, 0, 2):
        weight = jnp.concatenate([w_ref[a * 3 + b] for a in range(3)], axis=0)
        part = jnp.dot(rows_of_k, weight, preferred_element_type=jnp.float32)
        if b == 1:
            total = part
            continue
        column = lax.broadcasted_iota(jnp.int32, part.shape, 0) % width
        if b == 0:
            total = total + jnp.where(column == 0, 0.0, pltpu.roll(part, 1, 0))
        else:
            total = total + jnp.where(column == width - 1, 0.0, pltpu.roll(part, size - 1, 0))
    return total


def kernel(
    sections, bands, width,
    cur_in, skip_in, fresh_in, w1_in, ws_in, w2_in,
    produced_out, mirrored_out,
    w1, ws, w2, cur, mir, made, early, acc, hid,
    load_w, load_cur, load_mir, store_out,
    send_next, recv_next, send_mirror, recv_mirror,
    send_up, recv_below, send_down, recv_above,
    send_early, recv_early, send_outer, recv_outer,
):
    s = lax.axis_index("section")
    b = lax.axis_index("band")
    is_decoder = s >= sections // 2
    joined_encoder, joined_decoder = s == sections // 2 - 1, s == sections // 2
    sends_mirror = s < sections // 2 - 1
    takes_mirror = s > sections // 2
    ticks, images = made.shape[0], made.shape[1]
    own = made.shape[2]
    edge = HALO * width
    rows = own // width
    mirror = sections - 1 - s
    has_up, has_down = b > 0, b < bands - 1
    has_prev, has_next = s > 0, s < sections - 1
    middle = pl.ds(edge, own)
    above, below = pl.ds(0, edge), pl.ds(edge + own, edge)

    load_weights = [
        pltpu.make_async_copy(source, target, load_w.at[k])
        for k, (source, target) in enumerate(((w1_in, w1), (w2_in, w2), (ws_in, ws)))
    ]
    load_curs = [
        pltpu.make_async_copy(cur_in.at[i], cur.at[0, i, middle], load_cur.at[0, i])
        for i in range(images)
    ]
    load_mirs = [
        pltpu.make_async_copy(skip_in.at[i], mir.at[0, i, middle], load_mir.at[i])
        for i in range(images)
    ]
    load_fresh = {
        (t, i): pltpu.make_async_copy(
            fresh_in.at[t - 1, i], cur.at[t, i, middle], load_cur.at[t, i]
        )
        for t in range(1, ticks)
        for i in range(images)
    }
    load_curs[0].start()
    load_weights[0].start()
    load_weights[1].start()
    for copy in load_curs[1:]:
        copy.start()

    @pl.when(is_decoder)
    def _():
        load_weights[2].start()
        for copy in load_mirs:
            copy.start()

    @pl.when(s == 0)
    def _():
        for copy in load_fresh.values():
            copy.start()

    barrier = pltpu.get_barrier_semaphore()

    def greet(condition, device):
        @pl.when(condition)
        def _():
            pl.semaphore_signal(barrier, inc=1, device_id=device, device_id_type=MESH)

    greet(has_up, (s, b - 1))
    greet(has_down, (s, b + 1))
    greet(has_prev, (s - 1, b))
    greet(has_next, (s + 1, b))
    pl.semaphore_signal(barrier, inc=1, device_id=(mirror, b), device_id_type=MESH)

    blank = jnp.zeros((edge, cur.shape[3]), cur.dtype)

    @pl.when(jnp.logical_not(has_up))
    def _():
        for t in range(ticks):
            for i in range(images):
                cur[t, i, 0:edge] = blank
                mir[t, i, 0:edge] = blank

    @pl.when(jnp.logical_not(has_down))
    def _():
        for t in range(ticks):
            for i in range(images):
                cur[t, i, edge + own : edge + own + edge] = blank
                mir[t, i, edge + own : edge + own + edge] = blank

    greeted = (
        1
        + has_up.astype(jnp.int32)
        + has_down.astype(jnp.int32)
        + has_prev.astype(jnp.int32)
        + has_next.astype(jnp.int32)
    )

    inside = rows - 2 * HALO

    def make_early(i):
        load_curs[i].wait()
        if i == 0:
            load_weights[0].wait()
        part = conv_rows(cur[0, i, edge : edge + own], w1, inside + 2, width)
        hid[0 : (inside + 2) * width] = jnp.maximum(part, 0.0).astype(hid.dtype)
        if i == 0:
            load_weights[1].wait()
        part = conv_rows(hid[0 : (inside + 2) * width], w2, inside, width)
        early[i] = jnp.maximum(part, 0.0).astype(early.dtype)

    def to_mirror_early(i):
        return pltpu.make_async_remote_copy(
            src_ref=early.at[i],
            dst_ref=mir.at[1, i, pl.ds(2 * edge, inside * width)],
            send_sem=send_early.at[i],
            recv_sem=recv_early.at[i],
            device_id=(mirror, b),
            device_id_type=MESH,
        )

    @pl.when(sends_mirror)
    def _():
        make_early(0)

    pl.semaphore_wait(barrier, greeted)

    @pl.when(sends_mirror)
    def _():
        to_mirror_early(0).start()

    def to_up(kind, array, t, i, source):
        return pltpu.make_async_remote_copy(
            src_ref=source,
            dst_ref=array.at[t, i, below],
            send_sem=send_up.at[kind, t, i],
            recv_sem=recv_below.at[kind, t, i],
            device_id=(s, b - 1),
            device_id_type=MESH,
        )

    def to_down(kind, array, t, i, source):
        return pltpu.make_async_remote_copy(
            src_ref=source,
            dst_ref=array.at[t, i, above],
            send_sem=send_down.at[kind, t, i],
            recv_sem=recv_above.at[kind, t, i],
            device_id=(s, b + 1),
            device_id_type=MESH,
        )

    def give_edges(kind, array, t, i, source, first):
        @pl.when(has_up)
        def _():
            to_up(kind, array, t, i, source.at[pl.ds(first, edge)]).start()

        @pl.when(has_down)
        def _():
            to_down(kind, array, t, i, source.at[pl.ds(first + own - edge, edge)]).start()

    def await_edges(kind, array, t, i):
        @pl.when(has_up)
        def _():
            to_down(kind, array, t, i, array.at[t, i, above]).wait_recv()

        @pl.when(has_down)
        def _():
            to_up(kind, array, t, i, array.at[t, i, below]).wait_recv()

    def finish_edges(kind, array, t, i):
        @pl.when(has_up)
        def _():
            to_up(kind, array, t, i, array.at[t, i, above]).wait_send()

        @pl.when(has_down)
        def _():
            to_down(kind, array, t, i, array.at[t, i, below]).wait_send()

    def to_next(t, i):
        return pltpu.make_async_remote_copy(
            src_ref=made.at[t, i],
            dst_ref=cur.at[t + 1, i, middle],
            send_sem=send_next.at[t, i],
            recv_sem=recv_next.at[t, i],
            device_id=(s + 1, b),
            device_id_type=MESH,
        )

    def to_mirror(t, i):
        last = t + 1 == ticks
        return pltpu.make_async_remote_copy(
            src_ref=made.at[t, i],
            dst_ref=mirrored_out.at[i] if last else mir.at[t + 1, i, middle],
            send_sem=send_mirror.at[t, i],
            recv_sem=recv_mirror.at[t, i],
            device_id=(mirror, b),
            device_id_type=MESH,
        )

    def mirror_copies(t, i):
        if t > 0:
            return [to_mirror(t, i)]
        return [
            pltpu.make_async_remote_copy(
                src_ref=made.at[t, i, pl.ds(first, edge)],
                dst_ref=mir.at[t + 1, i, pl.ds(edge + first, edge)],
                send_sem=send_outer.at[k, i],
                recv_sem=recv_outer.at[k, i],
                device_id=(mirror, b),
                device_id_type=MESH,
            )
            for k, first in enumerate((0, own - edge))
        ]

    for i in range(images):
        give_edges(0, cur, 0, i, cur_in.at[i], 0)

        @pl.when(is_decoder)
        def _():
            give_edges(1, mir, 0, i, skip_in.at[i], 0)

    @pl.when(s == 0)
    def _():
        for t in range(1, ticks):
            for i in range(images):
                give_edges(0, cur, t, i, fresh_in.at[t - 1, i], 0)

    @pl.when(sends_mirror)
    def _():
        for i in range(1, images):
            make_early(i)
            to_mirror_early(i).start()

    inner = [(t, i) for i in range(images) for t in range(ticks - 1)]
    outer = [(ticks - 1, i) for i in range(images)]
    pending = list(inner)
    computed = set()
    in_flight = []

    def advance_mirrors():
        while pending and pending[0] in computed:
            step = pending.pop(0)

            @pl.when(sends_mirror)
            def _():
                if in_flight:
                    for copy in mirror_copies(*in_flight[-1]):
                        copy.wait_send()
                else:
                    for i in range(images):
                        to_mirror_early(i).wait_send()
                for copy in mirror_copies(*step):
                    copy.start()

            @pl.when(joined_encoder)
            def _():
                if in_flight:
                    to_next(*in_flight[-1]).wait_send()
                to_next(*step).start()

            in_flight.append(step)

    steps = [(0, i) for i in range(images)]
    steps += [(t, i) for i in range(images) for t in range(1, ticks)]
    for t, i in steps:
        if t == 0:

            @pl.when(jnp.logical_not(sends_mirror))
            def _():
                load_curs[i].wait()

        else:

            @pl.when(s == 0)
            def _():
                load_fresh[t, i].wait()

            @pl.when(has_prev)
            def _():
                to_next(t - 1, i).wait_recv()
                give_edges(0, cur, t, i, cur.at[t, i], edge)

        if t == 0 and i == 0:

            @pl.when(jnp.logical_not(sends_mirror))
            def _():
                load_weights[0].wait()
                load_weights[1].wait()

        await_edges(0, cur, t, i)
        acc[...] = conv_rows(cur[t, i], w1, rows + HALO, width)

        @pl.when(is_decoder)
        def _():
            if t == 0:
                if i == 0:
                    load_weights[2].wait()
                load_mirs[i].wait()
                await_edges(1, mir, t, i)
            else:

                @pl.when(takes_mirror)
                def _():
                    if t == 1:
                        to_mirror_early(i).wait_recv()
                    for copy in mirror_copies(t - 1, i):
                        copy.wait_recv()
                    give_edges(1, mir, t, i, mir.at[t, i], edge)
                    await_edges(1, mir, t, i)

                @pl.when(joined_decoder)
                def _():
                    mir[t, i] = cur[t, i]

            acc[...] += conv_rows(mir[t, i], ws, rows + HALO, width)

        hid[...] = jnp.maximum(acc[...], 0.0).astype(hid.dtype)
        nothing = jnp.zeros((width, hid.shape[1]), hid.dtype)

        @pl.when(jnp.logical_not(has_up))
        def _():
            hid[0:width] = nothing

        @pl.when(jnp.logical_not(has_down))
        def _():
            hid[width + own : width + own + width] = nothing

        made[t, i] = jnp.maximum(conv_rows(hid[...], w2, rows, width), 0.0).astype(made.dtype)
        if t + 1 < ticks:

            @pl.when(jnp.logical_and(has_next, jnp.logical_not(joined_encoder)))
            def _():
                to_next(t, i).start()

            computed.add((t, i))
            advance_mirrors()
        else:

            @pl.when(is_decoder)
            def _():
                to_mirror(t, i).start()

            pltpu.make_async_copy(made.at[t, i], produced_out.at[i], store_out.at[i]).start()

    @pl.when(jnp.logical_not(is_decoder))
    def _():
        for k, step in enumerate(outer):
            if k == 0:

                @pl.when(sends_mirror)
                def _():
                    for copy in mirror_copies(*in_flight[-1]):
                        copy.wait_send()

                @pl.when(joined_encoder)
                def _():
                    to_next(*in_flight[-1]).wait_send()

                to_mirror(*step).wait_recv()
            else:
                to_mirror(*outer[k - 1]).wait_send()
            to_mirror(*step).start()

        to_mirror(*outer[-1]).wait_send()
        for step in outer[1:]:
            to_mirror(*step).wait_recv()

    @pl.when(is_decoder)
    def _():
        for step in outer:
            to_mirror(*step).wait_send()
            to_mirror(*step).wait_recv()

    for i in range(images):
        pltpu.make_async_copy(made.at[ticks - 1, i], produced_out.at[i], store_out.at[i]).wait()
        for t in range(ticks):
            finish_edges(0, cur, t, i)

            @pl.when(is_decoder if t == 0 else takes_mirror)
            def _():
                finish_edges(1, mir, t, i)

            if t + 1 < ticks:

                @pl.when(jnp.logical_and(has_next, jnp.logical_not(joined_encoder)))
                def _():
                    to_next(t, i).wait_send()


def body(section_inputs, skip_inputs, fresh_batches, first_weights, skip_weights, second_weights):
    sections = lax.axis_size("section")
    bands = lax.axis_size("band")
    _, images, rows, width, channels = section_inputs.shape
    ticks = fresh_batches.shape[0] + 1
    own = rows * width
    padded = (rows + 2 * HALO) * width
    dtype = section_inputs.dtype
    out = jax.ShapeDtypeStruct((images, own, channels), dtype)
    taps = (9, channels, channels)
    dma = pltpu.SemaphoreType.DMA
    flops = 2 * ticks * images * own * 9 * channels * channels * 3
    produced, mirrored = pl.pallas_call(
        functools.partial(kernel, sections, bands, width),
        out_shape=(out, out),
        in_specs=[pl.BlockSpec(memory_space=pltpu.HBM)] * 6,
        out_specs=(pl.BlockSpec(memory_space=pltpu.HBM),) * 2,
        scratch_shapes=[
            pltpu.VMEM(taps, dtype),
            pltpu.VMEM(taps, dtype),
            pltpu.VMEM(taps, dtype),
            pltpu.VMEM((ticks, images, padded, channels), dtype),
            pltpu.VMEM((ticks, images, padded, channels), dtype),
            pltpu.VMEM((ticks, images, own, channels), dtype),
            pltpu.VMEM((images, own - 2 * HALO * width, channels), dtype),
            pltpu.VMEM(((rows + HALO) * width, channels), jnp.float32),
            pltpu.VMEM(((rows + HALO) * width, channels), dtype),
            dma((3,)),
            dma((ticks, images)),
            dma((images,)),
            dma((images,)),
            dma((ticks, images)),
            dma((ticks, images)),
            dma((ticks, images)),
            dma((ticks, images)),
            dma((2, ticks, images)),
            dma((2, ticks, images)),
            dma((2, ticks, images)),
            dma((2, ticks, images)),
            dma((images,)),
            dma((images,)),
            dma((2, images)),
            dma((2, images)),
        ],
        compiler_params=pltpu.CompilerParams(
            collective_id=0, has_side_effects=True, vmem_limit_bytes=63 * 1024 * 1024
        ),
        cost_estimate=pl.CostEstimate(flops=flops, bytes_accessed=8 * 2**20, transcendentals=0),
    )(
        section_inputs.reshape(images, own, channels),
        skip_inputs.reshape(images, own, channels),
        fresh_batches.reshape(ticks - 1, images, own, channels),
        first_weights.reshape(taps),
        skip_weights.reshape(taps),
        second_weights.reshape(taps),
    )
    shape = section_inputs.shape
    return produced.reshape(shape), mirrored.reshape(shape)


def solution(mesh):
    in_specs = (
        P("section", None, "band", None, None),
        P("section", None, "band", None, None),
        P(None, None, "band", None, None),
        P("section", None, None, None, None),
        P("section", None, None, None, None),
        P("section", None, None, None, None),
    )
    out_specs = (P("section", None, "band", None, None), P("section", None, "band", None, None))
    return jax.shard_map(body, mesh=mesh, in_specs=in_specs, out_specs=out_specs, check_vma=False)
```

```python
import functools

import jax
import jax.numpy as jnp
from jax import lax
from jax.experimental import pallas as pl
from jax.experimental.pallas import tpu as pltpu
from jax.sharding import PartitionSpec as P

MESH = pl.DeviceIdType.MESH
HALO = 2


def conv_rows(x, w_ref, out_rows, width):
    size = out_rows * width
    rows_of_k = jnp.concatenate([x[a * width : a * width + size] for a in range(3)], axis=1)
    total = None
    for b in (1, 0, 2):
        weight = jnp.concatenate([w_ref[a * 3 + b] for a in range(3)], axis=0)
        part = jnp.dot(rows_of_k, weight, preferred_element_type=jnp.float32)
        if b == 1:
            total = part
            continue
        column = lax.broadcasted_iota(jnp.int32, part.shape, 0) % width
        if b == 0:
            total = total + jnp.where(column == 0, 0.0, pltpu.roll(part, 1, 0))
        else:
            total = total + jnp.where(column == width - 1, 0.0, pltpu.roll(part, size - 1, 0))
    return total


def kernel(
    sections, bands, width,
    cur_in, skip_in, fresh_in, w1_in, ws_in, w2_in,
    produced_out, mirrored_out,
    w1, ws, w2, cur, mir, made, early, acc, hid,
    load_w, load_cur, load_mir, store_out,
    send_next, recv_next, send_mirror, recv_mirror,
    send_up, recv_below, send_down, recv_above,
    send_early, recv_early, send_outer, recv_outer,
):
    s = lax.axis_index("section")
    b = lax.axis_index("band")
    is_decoder = s >= sections // 2
    joined_encoder, joined_decoder = s == sections // 2 - 1, s == sections // 2
    sends_mirror = s < sections // 2 - 1
    takes_mirror = s > sections // 2
    before_last = s < sections - 1
    sends_early = jnp.logical_and(sends_mirror, s > 0) if made.shape[0] > 2 else sends_mirror
    ticks, images = made.shape[0], made.shape[1]
    own = made.shape[2]
    edge = HALO * width
    rows = own // width
    mirror = sections - 1 - s
    has_up, has_down = b > 0, b < bands - 1
    has_prev, has_next = s > 0, s < sections - 1
    middle = pl.ds(edge, own)
    above, below = pl.ds(0, edge), pl.ds(edge + own, edge)

    load_weights = [
        pltpu.make_async_copy(source, target, load_w.at[k])
        for k, (source, target) in enumerate(((w1_in, w1), (w2_in, w2), (ws_in, ws)))
    ]
    load_curs = [
        pltpu.make_async_copy(cur_in.at[i], cur.at[0, i, middle], load_cur.at[0, i])
        for i in range(images)
    ]
    load_mirs = [
        pltpu.make_async_copy(skip_in.at[i], mir.at[0, i, middle], load_mir.at[i])
        for i in range(images)
    ]
    load_fresh = {
        (t, i): pltpu.make_async_copy(
            fresh_in.at[t - 1, i], cur.at[t, i, middle], load_cur.at[t, i]
        )
        for t in range(1, ticks)
        for i in range(images)
    }
    load_curs[0].start()
    load_weights[0].start()
    load_weights[1].start()
    for copy in load_curs[1:]:
        copy.start()

    @pl.when(is_decoder)
    def _():
        load_weights[2].start()
        for copy in load_mirs:
            copy.start()

    @pl.when(s == 0)
    def _():
        for copy in load_fresh.values():
            copy.start()

    barrier = pltpu.get_barrier_semaphore()

    def greet(condition, device):
        @pl.when(condition)
        def _():
            pl.semaphore_signal(barrier, inc=1, device_id=device, device_id_type=MESH)

    greet(has_up, (s, b - 1))
    greet(has_down, (s, b + 1))
    greet(has_prev, (s - 1, b))
    greet(has_next, (s + 1, b))
    pl.semaphore_signal(barrier, inc=1, device_id=(mirror, b), device_id_type=MESH)

    blank = jnp.zeros((edge, cur.shape[3]), cur.dtype)

    @pl.when(jnp.logical_not(has_up))
    def _():
        for t in range(ticks):
            for i in range(images):
                cur[t, i, 0:edge] = blank
                mir[t, i, 0:edge] = blank

    @pl.when(jnp.logical_not(has_down))
    def _():
        for t in range(ticks):
            for i in range(images):
                cur[t, i, edge + own : edge + own + edge] = blank
                mir[t, i, edge + own : edge + own + edge] = blank

    greeted = (
        1
        + has_up.astype(jnp.int32)
        + has_down.astype(jnp.int32)
        + has_prev.astype(jnp.int32)
        + has_next.astype(jnp.int32)
    )

    inside = rows - 2 * HALO

    def make_early(i):
        load_curs[i].wait()
        if i == 0:
            load_weights[0].wait()
        part = conv_rows(cur[0, i, edge : edge + own], w1, inside + 2, width)
        hid[0 : (inside + 2) * width] = jnp.maximum(part, 0.0).astype(hid.dtype)
        if i == 0:
            load_weights[1].wait()
        part = conv_rows(hid[0 : (inside + 2) * width], w2, inside, width)
        early[i] = jnp.maximum(part, 0.0).astype(early.dtype)

    def to_mirror_early(i):
        return pltpu.make_async_remote_copy(
            src_ref=early.at[i],
            dst_ref=mir.at[1, i, pl.ds(2 * edge, inside * width)],
            send_sem=send_early.at[i],
            recv_sem=recv_early.at[i],
            device_id=(mirror, b),
            device_id_type=MESH,
        )

    @pl.when(sends_early)
    def _():
        make_early(0)

    pl.semaphore_wait(barrier, greeted)

    @pl.when(sends_early)
    def _():
        to_mirror_early(0).start()

    def to_up(kind, array, t, i, source):
        return pltpu.make_async_remote_copy(
            src_ref=source,
            dst_ref=array.at[t, i, below],
            send_sem=send_up.at[kind, t, i],
            recv_sem=recv_below.at[kind, t, i],
            device_id=(s, b - 1),
            device_id_type=MESH,
        )

    def to_down(kind, array, t, i, source):
        return pltpu.make_async_remote_copy(
            src_ref=source,
            dst_ref=array.at[t, i, above],
            send_sem=send_down.at[kind, t, i],
            recv_sem=recv_above.at[kind, t, i],
            device_id=(s, b + 1),
            device_id_type=MESH,
        )

    def give_edges(kind, array, t, i, source, first):
        @pl.when(has_up)
        def _():
            to_up(kind, array, t, i, source.at[pl.ds(first, edge)]).start()

        @pl.when(has_down)
        def _():
            to_down(kind, array, t, i, source.at[pl.ds(first + own - edge, edge)]).start()

    def await_edges(kind, array, t, i):
        @pl.when(has_up)
        def _():
            to_down(kind, array, t, i, array.at[t, i, above]).wait_recv()

        @pl.when(has_down)
        def _():
            to_up(kind, array, t, i, array.at[t, i, below]).wait_recv()

    def finish_edges(kind, array, t, i):
        @pl.when(has_up)
        def _():
            to_up(kind, array, t, i, array.at[t, i, above]).wait_send()

        @pl.when(has_down)
        def _():
            to_down(kind, array, t, i, array.at[t, i, below]).wait_send()

    def to_next(t, i):
        return pltpu.make_async_remote_copy(
            src_ref=made.at[t, i],
            dst_ref=cur.at[t + 1, i, middle],
            send_sem=send_next.at[t, i],
            recv_sem=recv_next.at[t, i],
            device_id=(s + 1, b),
            device_id_type=MESH,
        )

    def to_mirror(t, i):
        last = t + 1 == ticks
        return pltpu.make_async_remote_copy(
            src_ref=made.at[t, i],
            dst_ref=mirrored_out.at[i] if last else mir.at[t + 1, i, middle],
            send_sem=send_mirror.at[t, i],
            recv_sem=recv_mirror.at[t, i],
            device_id=(mirror, b),
            device_id_type=MESH,
        )

    def sends_next(t):
        reader = has_next if t == ticks - 2 else s < sections - 2
        return jnp.logical_and(reader, jnp.logical_not(joined_encoder))

    def mirror_copies(t, i):
        if t > 0:
            return [to_mirror(t, i)]
        return [
            pltpu.make_async_remote_copy(
                src_ref=made.at[t, i, pl.ds(first, edge)],
                dst_ref=mir.at[t + 1, i, pl.ds(edge + first, edge)],
                send_sem=send_outer.at[k, i],
                recv_sem=recv_outer.at[k, i],
                device_id=(mirror, b),
                device_id_type=MESH,
            )
            for k, first in enumerate((0, own - edge))
        ]

    for i in range(images):
        give_edges(0, cur, 0, i, cur_in.at[i], 0)

        @pl.when(is_decoder)
        def _():
            give_edges(1, mir, 0, i, skip_in.at[i], 0)

    @pl.when(s == 0)
    def _():
        for t in range(1, ticks):
            for i in range(images):
                give_edges(0, cur, t, i, fresh_in.at[t - 1, i], 0)

    @pl.when(sends_early)
    def _():
        for i in range(1, images):
            make_early(i)
            to_mirror_early(i).start()

    inner = [(t, i) for i in range(images) for t in range(ticks - 1)]
    outer = [(ticks - 1, i) for i in range(images)]
    order = [None] + inner + outer
    pending = list(inner)
    computed = set()

    def each_send(step, act):
        if step is None:

            @pl.when(sends_early)
            def _():
                for i in range(images):
                    act(to_mirror_early(i))

        elif step in outer:
            act(to_mirror(*step))
        else:

            @pl.when(sends_mirror if step[0] == ticks - 2 else sends_early)
            def _():
                for copy in mirror_copies(*step):
                    act(copy)

            @pl.when(joined_encoder)
            def _():
                act(to_next(*step))

    def begin(step):
        if order.index(step) >= 2:
            each_send(order[order.index(step) - 2], lambda copy: copy.wait_send())
        each_send(step, lambda copy: copy.start())

    def advance_mirrors():
        while pending and pending[0] in computed:
            begin(pending.pop(0))

    steps = [(0, i) for i in range(images)]
    steps += [(t, i) for i in range(images) for t in range(1, ticks)]
    def run_step(t, i):
        if t == 0:

            @pl.when(jnp.logical_not(sends_early))
            def _():
                load_curs[i].wait()

        else:

            @pl.when(s == 0)
            def _():
                load_fresh[t, i].wait()

            @pl.when(has_prev)
            def _():
                to_next(t - 1, i).wait_recv()
                give_edges(0, cur, t, i, cur.at[t, i], edge)

        if t == 0 and i == 0:

            @pl.when(jnp.logical_not(sends_early))
            def _():
                load_weights[0].wait()
                load_weights[1].wait()

        await_edges(0, cur, t, i)
        acc[...] = conv_rows(cur[t, i], w1, rows + HALO, width)

        @pl.when(is_decoder)
        def _():
            if t == 0:
                if i == 0:
                    load_weights[2].wait()
                load_mirs[i].wait()
                await_edges(1, mir, t, i)
            else:

                @pl.when(takes_mirror)
                def _():
                    if t == 1:
                        to_mirror_early(i).wait_recv()
                    for copy in mirror_copies(t - 1, i):
                        copy.wait_recv()
                    give_edges(1, mir, t, i, mir.at[t, i], edge)
                    await_edges(1, mir, t, i)

                @pl.when(joined_decoder)
                def _():
                    mir[t, i] = cur[t, i]

            acc[...] += conv_rows(mir[t, i], ws, rows + HALO, width)

        hid[...] = jnp.maximum(acc[...], 0.0).astype(hid.dtype)
        nothing = jnp.zeros((width, hid.shape[1]), hid.dtype)

        @pl.when(jnp.logical_not(has_up))
        def _():
            hid[0:width] = nothing

        @pl.when(jnp.logical_not(has_down))
        def _():
            hid[width + own : width + own + width] = nothing

        made[t, i] = jnp.maximum(conv_rows(hid[...], w2, rows, width), 0.0).astype(made.dtype)
        if t + 1 < ticks:

            @pl.when(sends_next(t))
            def _():
                to_next(t, i).start()

            computed.add((t, i))
            @pl.when(jnp.logical_not(is_decoder))
            def _():
                advance_mirrors()

        else:

            @pl.when(is_decoder)
            def _():
                to_mirror(t, i).start()

            pltpu.make_async_copy(made.at[t, i], produced_out.at[i], store_out.at[i]).start()

    for t, i in steps:
        if 0 < t < ticks - 1:

            @pl.when(before_last)
            def _():
                run_step(t, i)

        else:
            run_step(t, i)

    @pl.when(jnp.logical_not(is_decoder))
    def _():
        for k, step in enumerate(outer):
            if k == 0:
                to_mirror(*step).wait_recv()
            begin(step)

        for step in order[-2:]:
            each_send(step, lambda copy: copy.wait_send())
        for step in outer[1:]:
            to_mirror(*step).wait_recv()

    @pl.when(is_decoder)
    def _():
        for step in outer:
            to_mirror(*step).wait_send()
            to_mirror(*step).wait_recv()

    for i in range(images):
        pltpu.make_async_copy(made.at[ticks - 1, i], produced_out.at[i], store_out.at[i]).wait()
        for t in range(ticks):
            skipped = 0 < t < ticks - 1

            @pl.when(before_last if skipped else s >= 0)
            def _():
                finish_edges(0, cur, t, i)

            takes = jnp.logical_and(takes_mirror, before_last) if skipped else takes_mirror

            @pl.when(is_decoder if t == 0 else takes)
            def _():
                finish_edges(1, mir, t, i)

            if t + 1 < ticks:

                @pl.when(sends_next(t))
                def _():
                    to_next(t, i).wait_send()


def body(section_inputs, skip_inputs, fresh_batches, first_weights, skip_weights, second_weights):
    sections = lax.axis_size("section")
    bands = lax.axis_size("band")
    _, images, rows, width, channels = section_inputs.shape
    ticks = fresh_batches.shape[0] + 1
    own = rows * width
    padded = (rows + 2 * HALO) * width
    dtype = section_inputs.dtype
    out = jax.ShapeDtypeStruct((images, own, channels), dtype)
    taps = (9, channels, channels)
    dma = pltpu.SemaphoreType.DMA
    flops = 2 * ticks * images * own * 9 * channels * channels * 3
    produced, mirrored = pl.pallas_call(
        functools.partial(kernel, sections, bands, width),
        out_shape=(out, out),
        in_specs=[pl.BlockSpec(memory_space=pltpu.HBM)] * 6,
        out_specs=(pl.BlockSpec(memory_space=pltpu.HBM),) * 2,
        scratch_shapes=[
            pltpu.VMEM(taps, dtype),
            pltpu.VMEM(taps, dtype),
            pltpu.VMEM(taps, dtype),
            pltpu.VMEM((ticks, images, padded, channels), dtype),
            pltpu.VMEM((ticks, images, padded, channels), dtype),
            pltpu.VMEM((ticks, images, own, channels), dtype),
            pltpu.VMEM((images, own - 2 * HALO * width, channels), dtype),
            pltpu.VMEM(((rows + HALO) * width, channels), jnp.float32),
            pltpu.VMEM(((rows + HALO) * width, channels), dtype),
            dma((3,)),
            dma((ticks, images)),
            dma((images,)),
            dma((images,)),
            dma((ticks, images)),
            dma((ticks, images)),
            dma((ticks, images)),
            dma((ticks, images)),
            dma((2, ticks, images)),
            dma((2, ticks, images)),
            dma((2, ticks, images)),
            dma((2, ticks, images)),
            dma((images,)),
            dma((images,)),
            dma((2, images)),
            dma((2, images)),
        ],
        compiler_params=pltpu.CompilerParams(
            collective_id=0, has_side_effects=True, vmem_limit_bytes=63 * 1024 * 1024
        ),
        cost_estimate=pl.CostEstimate(flops=flops, bytes_accessed=8 * 2**20, transcendentals=0),
    )(
        section_inputs.reshape(images, own, channels),
        skip_inputs.reshape(images, own, channels),
        fresh_batches.reshape(ticks - 1, images, own, channels),
        first_weights.reshape(taps),
        skip_weights.reshape(taps),
        second_weights.reshape(taps),
    )
    shape = section_inputs.shape
    return produced.reshape(shape), mirrored.reshape(shape)


def solution(mesh):
    in_specs = (
        P("section", None, "band", None, None),
        P("section", None, "band", None, None),
        P(None, None, "band", None, None),
        P("section", None, None, None, None),
        P("section", None, None, None, None),
        P("section", None, None, None, None),
    )
    out_specs = (P("section", None, "band", None, None), P("section", None, "band", None, None))
    return jax.shard_map(body, mesh=mesh, in_specs=in_specs, out_specs=out_specs, check_vma=False)
```

```python
import functools

import jax
import jax.numpy as jnp
from jax import lax
from jax.experimental import pallas as pl
from jax.experimental.pallas import tpu as pltpu
from jax.sharding import PartitionSpec as P

MESH = pl.DeviceIdType.MESH
HALO = 2


def conv_rows(x, w_ref, out_rows, width):
    size = out_rows * width
    rows_of_k = jnp.concatenate([x[a * width : a * width + size] for a in range(3)], axis=1)
    total = None
    for b in (1, 0, 2):
        weight = jnp.concatenate([w_ref[a * 3 + b] for a in range(3)], axis=0)
        part = jnp.dot(rows_of_k, weight, preferred_element_type=jnp.float32)
        if b == 1:
            total = part
            continue
        column = lax.broadcasted_iota(jnp.int32, part.shape, 0) % width
        if b == 0:
            total = total + jnp.where(column == 0, 0.0, pltpu.roll(part, 1, 0))
        else:
            total = total + jnp.where(column == width - 1, 0.0, pltpu.roll(part, size - 1, 0))
    return total


def kernel(
    sections, bands, width,
    cur_in, skip_in, fresh_in, w1_in, ws_in, w2_in,
    produced_out, mirrored_out,
    w1, ws, w2, cur, mir, made, early, acc, hid,
    load_w, load_cur, load_mir, store_out,
    send_next, recv_next, send_mirror, recv_mirror,
    send_up, recv_below, send_down, recv_above,
    send_early, recv_early, send_outer, recv_outer, abreast,
):
    s = lax.axis_index("section")
    b = lax.axis_index("band")
    is_decoder = s >= sections // 2
    joined_encoder, joined_decoder = s == sections // 2 - 1, s == sections // 2
    sends_mirror = s < sections // 2 - 1
    takes_mirror = s > sections // 2
    before_last = s < sections - 1
    sends_early = jnp.logical_and(sends_mirror, s > 0) if made.shape[0] > 2 else sends_mirror
    ticks, images = made.shape[0], made.shape[1]
    own = made.shape[2]
    edge = HALO * width
    rows = own // width
    mirror = sections - 1 - s
    has_up, has_down = b > 0, b < bands - 1
    has_prev, has_next = s > 0, s < sections - 1
    middle = pl.ds(edge, own)
    above, below = pl.ds(0, edge), pl.ds(edge + own, edge)

    load_weights = [
        pltpu.make_async_copy(source, target, load_w.at[k])
        for k, (source, target) in enumerate(((w1_in, w1), (w2_in, w2), (ws_in, ws)))
    ]
    load_curs = [
        pltpu.make_async_copy(cur_in.at[i], cur.at[0, i, middle], load_cur.at[0, i])
        for i in range(images)
    ]
    load_mirs = [
        pltpu.make_async_copy(skip_in.at[i], mir.at[0, i, middle], load_mir.at[i])
        for i in range(images)
    ]
    load_fresh = {
        (t, i): pltpu.make_async_copy(
            fresh_in.at[t - 1, i], cur.at[t, i, middle], load_cur.at[t, i]
        )
        for t in range(1, ticks)
        for i in range(images)
    }
    load_curs[0].start()
    load_weights[0].start()
    load_weights[1].start()
    for copy in load_curs[1:]:
        copy.start()

    @pl.when(is_decoder)
    def _():
        load_weights[2].start()
        for copy in load_mirs:
            copy.start()

    @pl.when(s == 0)
    def _():
        for copy in load_fresh.values():
            copy.start()

    barrier = pltpu.get_barrier_semaphore()

    def greet(condition, device):
        @pl.when(condition)
        def _():
            pl.semaphore_signal(barrier, inc=1, device_id=device, device_id_type=MESH)

    greet(has_up, (s, b - 1))
    greet(has_down, (s, b + 1))
    greet(has_prev, (s - 1, b))
    greet(has_next, (s + 1, b))
    pl.semaphore_signal(barrier, inc=1, device_id=(mirror, b), device_id_type=MESH)

    other = s + 1 - 2 * (s % 2)
    across = s + 4 - 8 * ((s // 4) % 2)
    peers = [other, across, across + 1 - 2 * (s % 2)] if (sections // 2) % 8 == 0 else []
    for peer in peers:
        greet(jnp.logical_not(is_decoder), (peer, b))

    blank = jnp.zeros((edge, cur.shape[3]), cur.dtype)

    @pl.when(jnp.logical_not(has_up))
    def _():
        for t in range(ticks):
            for i in range(images):
                cur[t, i, 0:edge] = blank
                mir[t, i, 0:edge] = blank

    @pl.when(jnp.logical_not(has_down))
    def _():
        for t in range(ticks):
            for i in range(images):
                cur[t, i, edge + own : edge + own + edge] = blank
                mir[t, i, edge + own : edge + own + edge] = blank

    greeted = (
        1
        + has_up.astype(jnp.int32)
        + has_down.astype(jnp.int32)
        + has_prev.astype(jnp.int32)
        + has_next.astype(jnp.int32)
        + len(peers) * jnp.logical_not(is_decoder).astype(jnp.int32)
    )

    inside = rows - 2 * HALO

    def make_early(i):
        load_curs[i].wait()
        if i == 0:
            load_weights[0].wait()
        part = conv_rows(cur[0, i, edge : edge + own], w1, inside + 2, width)
        hid[0 : (inside + 2) * width] = jnp.maximum(part, 0.0).astype(hid.dtype)
        if i == 0:
            load_weights[1].wait()
        part = conv_rows(hid[0 : (inside + 2) * width], w2, inside, width)
        early[i] = jnp.maximum(part, 0.0).astype(early.dtype)

    def to_mirror_early(i):
        return pltpu.make_async_remote_copy(
            src_ref=early.at[i],
            dst_ref=mir.at[1, i, pl.ds(2 * edge, inside * width)],
            send_sem=send_early.at[i],
            recv_sem=recv_early.at[i],
            device_id=(mirror, b),
            device_id_type=MESH,
        )

    @pl.when(sends_early)
    def _():
        make_early(0)

    pl.semaphore_wait(barrier, greeted)

    @pl.when(sends_early)
    def _():
        to_mirror_early(0).start()

    def to_up(kind, array, t, i, source):
        return pltpu.make_async_remote_copy(
            src_ref=source,
            dst_ref=array.at[t, i, below],
            send_sem=send_up.at[kind, t, i],
            recv_sem=recv_below.at[kind, t, i],
            device_id=(s, b - 1),
            device_id_type=MESH,
        )

    def to_down(kind, array, t, i, source):
        return pltpu.make_async_remote_copy(
            src_ref=source,
            dst_ref=array.at[t, i, above],
            send_sem=send_down.at[kind, t, i],
            recv_sem=recv_above.at[kind, t, i],
            device_id=(s, b + 1),
            device_id_type=MESH,
        )

    def give_edges(kind, array, t, i, source, first):
        @pl.when(has_up)
        def _():
            to_up(kind, array, t, i, source.at[pl.ds(first, edge)]).start()

        @pl.when(has_down)
        def _():
            to_down(kind, array, t, i, source.at[pl.ds(first + own - edge, edge)]).start()

    def await_edges(kind, array, t, i):
        @pl.when(has_up)
        def _():
            to_down(kind, array, t, i, array.at[t, i, above]).wait_recv()

        @pl.when(has_down)
        def _():
            to_up(kind, array, t, i, array.at[t, i, below]).wait_recv()

    def finish_edges(kind, array, t, i):
        @pl.when(has_up)
        def _():
            to_up(kind, array, t, i, array.at[t, i, above]).wait_send()

        @pl.when(has_down)
        def _():
            to_down(kind, array, t, i, array.at[t, i, below]).wait_send()

    def to_next(t, i):
        return pltpu.make_async_remote_copy(
            src_ref=made.at[t, i],
            dst_ref=cur.at[t + 1, i, middle],
            send_sem=send_next.at[t, i],
            recv_sem=recv_next.at[t, i],
            device_id=(s + 1, b),
            device_id_type=MESH,
        )

    def to_mirror(t, i):
        last = t + 1 == ticks
        return pltpu.make_async_remote_copy(
            src_ref=made.at[t, i],
            dst_ref=mirrored_out.at[i] if last else mir.at[t + 1, i, middle],
            send_sem=send_mirror.at[t, i],
            recv_sem=recv_mirror.at[t, i],
            device_id=(mirror, b),
            device_id_type=MESH,
        )

    def sends_next(t):
        reader = has_next if t == ticks - 2 else s < sections - 2
        return jnp.logical_and(reader, jnp.logical_not(joined_encoder))

    def mirror_copies(t, i):
        if t > 0:
            return [to_mirror(t, i)]
        return [
            pltpu.make_async_remote_copy(
                src_ref=made.at[t, i, pl.ds(first, edge)],
                dst_ref=mir.at[t + 1, i, pl.ds(edge + first, edge)],
                send_sem=send_outer.at[k, i],
                recv_sem=recv_outer.at[k, i],
                device_id=(mirror, b),
                device_id_type=MESH,
            )
            for k, first in enumerate((0, own - edge))
        ]

    for i in range(images):
        give_edges(0, cur, 0, i, cur_in.at[i], 0)

        @pl.when(is_decoder)
        def _():
            give_edges(1, mir, 0, i, skip_in.at[i], 0)

    @pl.when(s == 0)
    def _():
        for t in range(1, ticks):
            for i in range(images):
                give_edges(0, cur, t, i, fresh_in.at[t - 1, i], 0)

    @pl.when(sends_early)
    def _():
        for i in range(1, images):
            make_early(i)
            to_mirror_early(i).start()

    inner = [(t, i) for i in range(images) for t in range(ticks - 1)]
    outer = [(ticks - 1, i) for i in range(images)]
    order = [None] + inner + outer
    pending = list(inner)
    computed = set()

    def each_send(step, act):
        if step is None:

            @pl.when(sends_early)
            def _():
                for i in range(images):
                    act(to_mirror_early(i))

        elif step in outer:
            act(to_mirror(*step))
        else:

            @pl.when(sends_mirror if step[0] == ticks - 2 else sends_early)
            def _():
                for copy in mirror_copies(*step):
                    act(copy)

            @pl.when(joined_encoder)
            def _():
                act(to_next(*step))

    def begin(step, gate=None):
        if order.index(step) >= 2:
            each_send(order[order.index(step) - 2], lambda copy: copy.wait_send())
        if gate is not None and peers:
            for peer in peers:
                pl.semaphore_signal(
                    abreast.at[gate], inc=1, device_id=(peer, b), device_id_type=MESH
                )
            pl.semaphore_wait(abreast.at[gate], len(peers))
        each_send(step, lambda copy: copy.start())

    def advance_mirrors():
        while pending and pending[0] in computed:
            begin(pending.pop(0))

    steps = [(0, i) for i in range(images)]
    steps += [(t, i) for i in range(images) for t in range(1, ticks)]
    def run_step(t, i):
        if t == 0:

            @pl.when(jnp.logical_not(sends_early))
            def _():
                load_curs[i].wait()

        else:

            @pl.when(s == 0)
            def _():
                load_fresh[t, i].wait()

            @pl.when(has_prev)
            def _():
                to_next(t - 1, i).wait_recv()
                give_edges(0, cur, t, i, cur.at[t, i], edge)

        if t == 0 and i == 0:

            @pl.when(jnp.logical_not(sends_early))
            def _():
                load_weights[0].wait()
                load_weights[1].wait()

        await_edges(0, cur, t, i)
        acc[...] = conv_rows(cur[t, i], w1, rows + HALO, width)

        @pl.when(is_decoder)
        def _():
            if t == 0:
                if i == 0:
                    load_weights[2].wait()
                load_mirs[i].wait()
                await_edges(1, mir, t, i)
            else:

                @pl.when(takes_mirror)
                def _():
                    if t == 1:
                        to_mirror_early(i).wait_recv()
                    for copy in mirror_copies(t - 1, i):
                        copy.wait_recv()
                    give_edges(1, mir, t, i, mir.at[t, i], edge)
                    await_edges(1, mir, t, i)

                @pl.when(joined_decoder)
                def _():
                    mir[t, i] = cur[t, i]

            acc[...] += conv_rows(mir[t, i], ws, rows + HALO, width)

        hid[...] = jnp.maximum(acc[...], 0.0).astype(hid.dtype)
        nothing = jnp.zeros((width, hid.shape[1]), hid.dtype)

        @pl.when(jnp.logical_not(has_up))
        def _():
            hid[0:width] = nothing

        @pl.when(jnp.logical_not(has_down))
        def _():
            hid[width + own : width + own + width] = nothing

        made[t, i] = jnp.maximum(conv_rows(hid[...], w2, rows, width), 0.0).astype(made.dtype)
        if t + 1 < ticks:

            @pl.when(sends_next(t))
            def _():
                to_next(t, i).start()

            computed.add((t, i))
            @pl.when(jnp.logical_not(is_decoder))
            def _():
                advance_mirrors()

        else:

            @pl.when(is_decoder)
            def _():
                to_mirror(t, i).start()

            pltpu.make_async_copy(made.at[t, i], produced_out.at[i], store_out.at[i]).start()

    for t, i in steps:
        if 0 < t < ticks - 1:

            @pl.when(before_last)
            def _():
                run_step(t, i)

        else:
            run_step(t, i)

    @pl.when(jnp.logical_not(is_decoder))
    def _():
        for k, step in enumerate(outer):
            begin(step, k)

        for step in order[-2:]:
            each_send(step, lambda copy: copy.wait_send())
        for step in outer:
            to_mirror(*step).wait_recv()

    @pl.when(is_decoder)
    def _():
        for step in outer:
            to_mirror(*step).wait_send()
            to_mirror(*step).wait_recv()

    for i in range(images):
        pltpu.make_async_copy(made.at[ticks - 1, i], produced_out.at[i], store_out.at[i]).wait()
        for t in range(ticks):
            skipped = 0 < t < ticks - 1

            @pl.when(before_last if skipped else s >= 0)
            def _():
                finish_edges(0, cur, t, i)

            takes = jnp.logical_and(takes_mirror, before_last) if skipped else takes_mirror

            @pl.when(is_decoder if t == 0 else takes)
            def _():
                finish_edges(1, mir, t, i)

            if t + 1 < ticks:

                @pl.when(sends_next(t))
                def _():
                    to_next(t, i).wait_send()


def body(section_inputs, skip_inputs, fresh_batches, first_weights, skip_weights, second_weights):
    sections = lax.axis_size("section")
    bands = lax.axis_size("band")
    _, images, rows, width, channels = section_inputs.shape
    ticks = fresh_batches.shape[0] + 1
    own = rows * width
    padded = (rows + 2 * HALO) * width
    dtype = section_inputs.dtype
    out = jax.ShapeDtypeStruct((images, own, channels), dtype)
    taps = (9, channels, channels)
    dma = pltpu.SemaphoreType.DMA
    flops = 2 * ticks * images * own * 9 * channels * channels * 3
    produced, mirrored = pl.pallas_call(
        functools.partial(kernel, sections, bands, width),
        out_shape=(out, out),
        in_specs=[pl.BlockSpec(memory_space=pltpu.HBM)] * 6,
        out_specs=(pl.BlockSpec(memory_space=pltpu.HBM),) * 2,
        scratch_shapes=[
            pltpu.VMEM(taps, dtype),
            pltpu.VMEM(taps, dtype),
            pltpu.VMEM(taps, dtype),
            pltpu.VMEM((ticks, images, padded, channels), dtype),
            pltpu.VMEM((ticks, images, padded, channels), dtype),
            pltpu.VMEM((ticks, images, own, channels), dtype),
            pltpu.VMEM((images, own - 2 * HALO * width, channels), dtype),
            pltpu.VMEM(((rows + HALO) * width, channels), jnp.float32),
            pltpu.VMEM(((rows + HALO) * width, channels), dtype),
            dma((3,)),
            dma((ticks, images)),
            dma((images,)),
            dma((images,)),
            dma((ticks, images)),
            dma((ticks, images)),
            dma((ticks, images)),
            dma((ticks, images)),
            dma((2, ticks, images)),
            dma((2, ticks, images)),
            dma((2, ticks, images)),
            dma((2, ticks, images)),
            dma((images,)),
            dma((images,)),
            dma((2, images)),
            dma((2, images)),
            pltpu.SemaphoreType.REGULAR((images,)),
        ],
        compiler_params=pltpu.CompilerParams(
            collective_id=0, has_side_effects=True, vmem_limit_bytes=63 * 1024 * 1024
        ),
        cost_estimate=pl.CostEstimate(flops=flops, bytes_accessed=8 * 2**20, transcendentals=0),
    )(
        section_inputs.reshape(images, own, channels),
        skip_inputs.reshape(images, own, channels),
        fresh_batches.reshape(ticks - 1, images, own, channels),
        first_weights.reshape(taps),
        skip_weights.reshape(taps),
        second_weights.reshape(taps),
    )
    shape = section_inputs.shape
    return produced.reshape(shape), mirrored.reshape(shape)


def solution(mesh):
    in_specs = (
        P("section", None, "band", None, None),
        P("section", None, "band", None, None),
        P(None, None, "band", None, None),
        P("section", None, None, None, None),
        P("section", None, None, None, None),
        P("section", None, None, None, None),
    )
    out_specs = (P("section", None, "band", None, None), P("section", None, "band", None, None))
    return jax.shard_map(body, mesh=mesh, in_specs=in_specs, out_specs=out_specs, check_vma=False)
```

```python
import functools

import jax
import jax.numpy as jnp
from jax import lax
from jax.experimental import pallas as pl
from jax.experimental.pallas import tpu as pltpu
from jax.sharding import PartitionSpec as P

MESH = pl.DeviceIdType.MESH
HALO = 2


def conv_rows(x, w_ref, out_rows, width):
    size = out_rows * width
    rows_of_k = jnp.concatenate([x[a * width : a * width + size] for a in range(3)], axis=1)
    total = None
    for b in (1, 0, 2):
        weight = jnp.concatenate([w_ref[a * 3 + b] for a in range(3)], axis=0)
        part = jnp.dot(rows_of_k, weight, preferred_element_type=jnp.float32)
        if b == 1:
            total = part
            continue
        column = lax.broadcasted_iota(jnp.int32, part.shape, 0) % width
        if b == 0:
            total = total + jnp.where(column == 0, 0.0, pltpu.roll(part, 1, 0))
        else:
            total = total + jnp.where(column == width - 1, 0.0, pltpu.roll(part, size - 1, 0))
    return total


def kernel(
    sections, bands, width,
    cur_in, skip_in, fresh_in, w1_in, ws_in, w2_in,
    produced_out, mirrored_out,
    w1, ws, w2, cur, mir, made, early, acc, hid,
    load_w, load_cur, load_mir, store_out,
    send_next, recv_next, send_mirror, recv_mirror,
    send_up, recv_below, send_down, recv_above,
    send_early, recv_early, send_outer, recv_outer, abreast,
):
    s = lax.axis_index("section")
    b = lax.axis_index("band")
    is_decoder = s >= sections // 2
    joined_encoder, joined_decoder = s == sections // 2 - 1, s == sections // 2
    sends_mirror = s < sections // 2 - 1
    takes_mirror = s > sections // 2
    before_last = s < sections - 1
    sends_early = jnp.logical_and(sends_mirror, s > 0) if made.shape[0] > 2 else sends_mirror
    ticks, images = made.shape[0], made.shape[1]
    own = made.shape[2]
    edge = HALO * width
    rows = own // width
    mirror = sections - 1 - s
    has_up, has_down = b > 0, b < bands - 1
    has_prev, has_next = s > 0, s < sections - 1
    middle = pl.ds(edge, own)
    above, below = pl.ds(0, edge), pl.ds(edge + own, edge)

    load_weights = [
        pltpu.make_async_copy(source, target, load_w.at[k])
        for k, (source, target) in enumerate(((w1_in, w1), (w2_in, w2), (ws_in, ws)))
    ]
    load_curs = [
        pltpu.make_async_copy(cur_in.at[i], cur.at[0, i, middle], load_cur.at[0, i])
        for i in range(images)
    ]
    load_mirs = [
        pltpu.make_async_copy(skip_in.at[i], mir.at[0, i, middle], load_mir.at[i])
        for i in range(images)
    ]
    load_fresh = {
        (t, i): pltpu.make_async_copy(
            fresh_in.at[t - 1, i], cur.at[t, i, middle], load_cur.at[t, i]
        )
        for t in range(1, ticks)
        for i in range(images)
    }
    load_curs[0].start()
    load_weights[0].start()
    load_weights[1].start()
    for copy in load_curs[1:]:
        copy.start()

    @pl.when(is_decoder)
    def _():
        load_weights[2].start()
        for copy in load_mirs:
            copy.start()

    @pl.when(s == 0)
    def _():
        for copy in load_fresh.values():
            copy.start()

    barrier = pltpu.get_barrier_semaphore()

    def greet(condition, device):
        @pl.when(condition)
        def _():
            pl.semaphore_signal(barrier, inc=1, device_id=device, device_id_type=MESH)

    greet(has_up, (s, b - 1))
    greet(has_down, (s, b + 1))
    greet(has_prev, (s - 1, b))
    greet(has_next, (s + 1, b))
    pl.semaphore_signal(barrier, inc=1, device_id=(mirror, b), device_id_type=MESH)

    other = s + 1 - 2 * (s % 2)
    across = s + 4 - 8 * ((s // 4) % 2)
    peers = [other, across, across + 1 - 2 * (s % 2)] if (sections // 2) % 8 == 0 else []
    for peer in peers:
        greet(jnp.logical_not(is_decoder), (peer, b))

    blank = jnp.zeros((edge, cur.shape[3]), cur.dtype)

    @pl.when(jnp.logical_not(has_up))
    def _():
        for t in range(ticks):
            for i in range(images):
                cur[t, i, 0:edge] = blank
                mir[t, i, 0:edge] = blank

    @pl.when(jnp.logical_not(has_down))
    def _():
        for t in range(ticks):
            for i in range(images):
                cur[t, i, edge + own : edge + own + edge] = blank
                mir[t, i, edge + own : edge + own + edge] = blank

    greeted = (
        1
        + has_up.astype(jnp.int32)
        + has_down.astype(jnp.int32)
        + has_prev.astype(jnp.int32)
        + has_next.astype(jnp.int32)
        + len(peers) * jnp.logical_not(is_decoder).astype(jnp.int32)
    )

    inside = rows - 2 * HALO

    def make_early(i):
        load_curs[i].wait()
        if i == 0:
            load_weights[0].wait()
        part = conv_rows(cur[0, i, edge : edge + own], w1, inside + 2, width)
        hid[0 : (inside + 2) * width] = jnp.maximum(part, 0.0).astype(hid.dtype)
        if i == 0:
            load_weights[1].wait()
        part = conv_rows(hid[0 : (inside + 2) * width], w2, inside, width)
        early[i] = jnp.maximum(part, 0.0).astype(early.dtype)

    def to_mirror_early(i):
        return pltpu.make_async_remote_copy(
            src_ref=early.at[i],
            dst_ref=mir.at[1, i, pl.ds(2 * edge, inside * width)],
            send_sem=send_early.at[i],
            recv_sem=recv_early.at[i],
            device_id=(mirror, b),
            device_id_type=MESH,
        )

    @pl.when(sends_early)
    def _():
        make_early(0)

    pl.semaphore_wait(barrier, greeted)

    @pl.when(sends_early)
    def _():
        to_mirror_early(0).start()

    def to_up(kind, array, t, i, source):
        return pltpu.make_async_remote_copy(
            src_ref=source,
            dst_ref=array.at[t, i, below],
            send_sem=send_up.at[kind, t, i],
            recv_sem=recv_below.at[kind, t, i],
            device_id=(s, b - 1),
            device_id_type=MESH,
        )

    def to_down(kind, array, t, i, source):
        return pltpu.make_async_remote_copy(
            src_ref=source,
            dst_ref=array.at[t, i, above],
            send_sem=send_down.at[kind, t, i],
            recv_sem=recv_above.at[kind, t, i],
            device_id=(s, b + 1),
            device_id_type=MESH,
        )

    def give_edges(kind, array, t, i, source, first):
        @pl.when(has_up)
        def _():
            to_up(kind, array, t, i, source.at[pl.ds(first, edge)]).start()

        @pl.when(has_down)
        def _():
            to_down(kind, array, t, i, source.at[pl.ds(first + own - edge, edge)]).start()

    def await_edges(kind, array, t, i):
        @pl.when(has_up)
        def _():
            to_down(kind, array, t, i, array.at[t, i, above]).wait_recv()

        @pl.when(has_down)
        def _():
            to_up(kind, array, t, i, array.at[t, i, below]).wait_recv()

    def finish_edges(kind, array, t, i):
        @pl.when(has_up)
        def _():
            to_up(kind, array, t, i, array.at[t, i, above]).wait_send()

        @pl.when(has_down)
        def _():
            to_down(kind, array, t, i, array.at[t, i, below]).wait_send()

    def to_next(t, i):
        return pltpu.make_async_remote_copy(
            src_ref=made.at[t, i],
            dst_ref=cur.at[t + 1, i, middle],
            send_sem=send_next.at[t, i],
            recv_sem=recv_next.at[t, i],
            device_id=(s + 1, b),
            device_id_type=MESH,
        )

    def to_mirror(t, i):
        last = t + 1 == ticks
        return pltpu.make_async_remote_copy(
            src_ref=made.at[t, i],
            dst_ref=mirrored_out.at[i] if last else mir.at[t + 1, i, middle],
            send_sem=send_mirror.at[t, i],
            recv_sem=recv_mirror.at[t, i],
            device_id=(mirror, b),
            device_id_type=MESH,
        )

    def sends_next(t):
        reader = has_next if t == ticks - 2 else s < sections - 2
        return jnp.logical_and(reader, jnp.logical_not(joined_encoder))

    def mirror_copies(t, i):
        if t > 0:
            return [to_mirror(t, i)]
        return [
            pltpu.make_async_remote_copy(
                src_ref=made.at[t, i, pl.ds(first, edge)],
                dst_ref=mir.at[t + 1, i, pl.ds(edge + first, edge)],
                send_sem=send_outer.at[k, i],
                recv_sem=recv_outer.at[k, i],
                device_id=(mirror, b),
                device_id_type=MESH,
            )
            for k, first in enumerate((0, own - edge))
        ]

    for i in range(images):
        give_edges(0, cur, 0, i, cur_in.at[i], 0)

        @pl.when(is_decoder)
        def _():
            give_edges(1, mir, 0, i, skip_in.at[i], 0)

    @pl.when(s == 0)
    def _():
        for t in range(1, ticks):
            for i in range(images):
                give_edges(0, cur, t, i, fresh_in.at[t - 1, i], 0)

    @pl.when(sends_early)
    def _():
        for i in range(1, images):
            make_early(i)
            to_mirror_early(i).start()

    inner = [(t, i) for i in range(images) for t in range(ticks - 1)]
    outer = [(ticks - 1, i) for i in range(images)]
    order = [None] + inner + outer
    pending = list(inner)
    computed = set()

    def each_send(step, act):
        if step is None:

            @pl.when(sends_early)
            def _():
                for i in range(images):
                    act(to_mirror_early(i))

        elif step in outer:
            act(to_mirror(*step))
        else:

            @pl.when(sends_mirror if step[0] == ticks - 2 else sends_early)
            def _():
                for copy in mirror_copies(*step):
                    act(copy)

            @pl.when(joined_encoder)
            def _():
                act(to_next(*step))

    def begin(step, gate=None):
        if order.index(step) >= 3:
            each_send(order[order.index(step) - 3], lambda copy: copy.wait_send())
        if gate is not None and peers:
            for peer in peers:
                pl.semaphore_signal(
                    abreast.at[gate], inc=1, device_id=(peer, b), device_id_type=MESH
                )
            pl.semaphore_wait(abreast.at[gate], len(peers))
        each_send(step, lambda copy: copy.start())

    def advance_mirrors():
        while pending and pending[0] in computed:
            begin(pending.pop(0))

    steps = [(0, i) for i in range(images)]
    steps += [(t, i) for i in range(images) for t in range(1, ticks)]
    def run_step(t, i):
        if t == 0:

            @pl.when(jnp.logical_not(sends_early))
            def _():
                load_curs[i].wait()

        else:

            @pl.when(s == 0)
            def _():
                load_fresh[t, i].wait()

            @pl.when(has_prev)
            def _():
                to_next(t - 1, i).wait_recv()
                give_edges(0, cur, t, i, cur.at[t, i], edge)

        if t == 0 and i == 0:

            @pl.when(jnp.logical_not(sends_early))
            def _():
                load_weights[0].wait()
                load_weights[1].wait()

        await_edges(0, cur, t, i)
        acc[...] = conv_rows(cur[t, i], w1, rows + HALO, width)

        @pl.when(is_decoder)
        def _():
            if t == 0:
                if i == 0:
                    load_weights[2].wait()
                load_mirs[i].wait()
                await_edges(1, mir, t, i)
            else:

                @pl.when(takes_mirror)
                def _():
                    if t == 1:
                        to_mirror_early(i).wait_recv()
                    for copy in mirror_copies(t - 1, i):
                        copy.wait_recv()
                    give_edges(1, mir, t, i, mir.at[t, i], edge)
                    await_edges(1, mir, t, i)

                @pl.when(joined_decoder)
                def _():
                    mir[t, i] = cur[t, i]

            acc[...] += conv_rows(mir[t, i], ws, rows + HALO, width)

        hid[...] = jnp.maximum(acc[...], 0.0).astype(hid.dtype)
        nothing = jnp.zeros((width, hid.shape[1]), hid.dtype)

        @pl.when(jnp.logical_not(has_up))
        def _():
            hid[0:width] = nothing

        @pl.when(jnp.logical_not(has_down))
        def _():
            hid[width + own : width + own + width] = nothing

        made[t, i] = jnp.maximum(conv_rows(hid[...], w2, rows, width), 0.0).astype(made.dtype)
        if t + 1 < ticks:

            @pl.when(sends_next(t))
            def _():
                to_next(t, i).start()

            computed.add((t, i))
            @pl.when(jnp.logical_not(is_decoder))
            def _():
                advance_mirrors()

        else:

            @pl.when(is_decoder)
            def _():
                to_mirror(t, i).start()

            pltpu.make_async_copy(made.at[t, i], produced_out.at[i], store_out.at[i]).start()

    for t, i in steps:
        if 0 < t < ticks - 1:

            @pl.when(before_last)
            def _():
                run_step(t, i)

        else:
            run_step(t, i)

    @pl.when(jnp.logical_not(is_decoder))
    def _():
        for k, step in enumerate(outer):
            begin(step, k)

        for step in order[-3:]:
            each_send(step, lambda copy: copy.wait_send())
        for step in outer:
            to_mirror(*step).wait_recv()

    @pl.when(is_decoder)
    def _():
        for step in outer:
            to_mirror(*step).wait_send()
            to_mirror(*step).wait_recv()

    for i in range(images):
        pltpu.make_async_copy(made.at[ticks - 1, i], produced_out.at[i], store_out.at[i]).wait()
        for t in range(ticks):
            skipped = 0 < t < ticks - 1

            @pl.when(before_last if skipped else s >= 0)
            def _():
                finish_edges(0, cur, t, i)

            takes = jnp.logical_and(takes_mirror, before_last) if skipped else takes_mirror

            @pl.when(is_decoder if t == 0 else takes)
            def _():
                finish_edges(1, mir, t, i)

            if t + 1 < ticks:

                @pl.when(sends_next(t))
                def _():
                    to_next(t, i).wait_send()


def body(section_inputs, skip_inputs, fresh_batches, first_weights, skip_weights, second_weights):
    sections = lax.axis_size("section")
    bands = lax.axis_size("band")
    _, images, rows, width, channels = section_inputs.shape
    ticks = fresh_batches.shape[0] + 1
    own = rows * width
    padded = (rows + 2 * HALO) * width
    dtype = section_inputs.dtype
    out = jax.ShapeDtypeStruct((images, own, channels), dtype)
    taps = (9, channels, channels)
    dma = pltpu.SemaphoreType.DMA
    flops = 2 * ticks * images * own * 9 * channels * channels * 3
    produced, mirrored = pl.pallas_call(
        functools.partial(kernel, sections, bands, width),
        out_shape=(out, out),
        in_specs=[pl.BlockSpec(memory_space=pltpu.HBM)] * 6,
        out_specs=(pl.BlockSpec(memory_space=pltpu.HBM),) * 2,
        scratch_shapes=[
            pltpu.VMEM(taps, dtype),
            pltpu.VMEM(taps, dtype),
            pltpu.VMEM(taps, dtype),
            pltpu.VMEM((ticks, images, padded, channels), dtype),
            pltpu.VMEM((ticks, images, padded, channels), dtype),
            pltpu.VMEM((ticks, images, own, channels), dtype),
            pltpu.VMEM((images, own - 2 * HALO * width, channels), dtype),
            pltpu.VMEM(((rows + HALO) * width, channels), jnp.float32),
            pltpu.VMEM(((rows + HALO) * width, channels), dtype),
            dma((3,)),
            dma((ticks, images)),
            dma((images,)),
            dma((images,)),
            dma((ticks, images)),
            dma((ticks, images)),
            dma((ticks, images)),
            dma((ticks, images)),
            dma((2, ticks, images)),
            dma((2, ticks, images)),
            dma((2, ticks, images)),
            dma((2, ticks, images)),
            dma((images,)),
            dma((images,)),
            dma((2, images)),
            dma((2, images)),
            pltpu.SemaphoreType.REGULAR((images,)),
        ],
        compiler_params=pltpu.CompilerParams(
            collective_id=0, has_side_effects=True, vmem_limit_bytes=63 * 1024 * 1024
        ),
        cost_estimate=pl.CostEstimate(flops=flops, bytes_accessed=8 * 2**20, transcendentals=0),
    )(
        section_inputs.reshape(images, own, channels),
        skip_inputs.reshape(images, own, channels),
        fresh_batches.reshape(ticks - 1, images, own, channels),
        first_weights.reshape(taps),
        skip_weights.reshape(taps),
        second_weights.reshape(taps),
    )
    shape = section_inputs.shape
    return produced.reshape(shape), mirrored.reshape(shape)


def solution(mesh):
    in_specs = (
        P("section", None, "band", None, None),
        P("section", None, "band", None, None),
        P(None, None, "band", None, None),
        P("section", None, None, None, None),
        P("section", None, None, None, None),
        P("section", None, None, None, None),
    )
    out_specs = (P("section", None, "band", None, None), P("section", None, "band", None, None))
    return jax.shard_map(body, mesh=mesh, in_specs=in_specs, out_specs=out_specs, check_vma=False)
```
